512 devices in a mesh: dp: 64 (over z, y), mp: 8 (over x, core).
Axes of the slice: x: 4, y: 8, z: 8, core: 2. Of those that a mesh axis runs over, the one named last changes fastest.
Arguments:
- inputs: bfloat16 [32768, 1024], P('dp', 'mp'), may hold values from -6 to 6
- out_grads: bfloat16 [32768, 8192], P('dp', 'mp'), may hold values from -0.03125 to 0.03125
- sketch: float32 [8, 1024, 256], P('mp', 'dp'), may hold values from -6 to 6
Outputs:
- update: float32 [8, 1024, 1024], P('mp', None, 'dp')
- new_sketch: float32 [8, 1024, 256], P('mp', 'dp')
The draws below stay inside these ranges and needn't reach their ends.
All inputs are finite; a program needn't handle non-finite values.
Results may differ from the reference program's by a relative error of at most 0.00045.
Values may be sent and summed in bfloat16 or wider, within the bound.
No kernel may reach another device: no remote copies, remote signals or barrier semaphores. Data moves between devices by JAX's collectives and lax.ppermute only.
A program may use at most 64 MiB of HBM per device.

```python
import jax
import jax.numpy as jnp
from jax import lax

BLOCK = 1024
RANK = 256
NS_ITERS = 8
TOKENS = 32768
COLS = 8192
N_MP = 8


def levels(own_key, shape, pieces, low, top_value):
    loudness = 1.0
    for dim, parts in pieces:
        draws = jax.random.uniform(jax.random.fold_in(jax.random.fold_in(own_key, 6), dim), (parts,), jnp.float32, low / len(pieces), top_value / len(pieces))
        loudness = loudness * jnp.repeat(jnp.exp(draws), shape[dim] // parts).reshape((-1,) + (1,) * (len(shape) - 1 - dim))
    return loudness


def centred(own_key, shape, deviation, limit, shards=(), held_as=jnp.bfloat16):
    values = jax.random.normal(own_key, shape, jnp.float32) * deviation
    if len(shards) > 0:
        values = levels(own_key, shape, shards, -0.22, 0.18) * values
    return jnp.clip(values, min=-limit, max=limit).astype(held_as)


def setup_inputs(seed: int = 0) -> dict:
    key_of = jax.random.split(jax.random.key(seed), 4)
    inputs = centred(key_of[0], (TOKENS, BLOCK), 1.0, 6.0, ((0, 64), (1, 8)))
    out_grads = centred(key_of[1], (TOKENS, COLS), TOKENS ** -0.5, 0.03125, ((0, 64), (1, 8)))
    sketch = centred(key_of[2], (N_MP, BLOCK, RANK), 1.0, 6.0, ((0, 8), (1, 64)), jnp.float32)
    return {"inputs": inputs, "out_grads": out_grads, "sketch": sketch}


def matmul(left, right):
    return jnp.dot(left, right, precision=lax.Precision.HIGHEST, preferred_element_type=jnp.float32)

def root_pair(matrix):
    order = matrix.shape[0]
    ident = jnp.eye(order, dtype=jnp.float32)
    scale = jnp.trace(matrix)
    ymat = matrix / scale
    zmat = ident
    for step in range(NS_ITERS):
        weight = 1.5 * ident - 0.5 * matmul(zmat, ymat)
        ymat, zmat = (matmul(ymat, weight), matmul(weight, zmat))
    return (jnp.sqrt(scale) * ymat, zmat / jnp.sqrt(scale))

def refresh(grad, sketch_block):
    ident = jnp.eye(RANK, dtype=jnp.float32)
    power = 0.95 * matmul(sketch_block, matmul(sketch_block.T, sketch_block)) + matmul(grad, matmul(grad.T, sketch_block))
    gram = matmul(power.T, power)
    spow = matmul(sketch_block.T, power)
    gpow = matmul(grad.T, power)
    ritz = 0.95 * matmul(spow.T, spow) + matmul(gpow.T, gpow)
    unused, cinv = root_pair(gram)
    hmat = matmul(matmul(cinv, ritz), cinv)
    eps = 0.1 * jnp.trace(hmat) / RANK
    root, rinv = root_pair(hmat + eps * ident)
    basis = matmul(power, cinv)
    fresh = matmul(basis, root)
    coef = matmul(basis.T, grad)
    update = grad + matmul(basis, matmul(jnp.sqrt(eps) * rinv - ident, coef))
    return (update, fresh)

def reference(inputs, out_grads, sketch):
    updates = []
    sketches = []
    for block in range(N_MP):
        columns = out_grads[:, block * BLOCK:(block + 1) * BLOCK]
        grad = jnp.dot(inputs.T, columns, preferred_element_type=jnp.float32)
        update, fresh = refresh(grad, sketch[block])
        updates.append(update)
        sketches.append(fresh)
    return (jnp.stack(updates), jnp.stack(sketches))
```

```python
import jax
import jax.numpy as jnp
from jax import lax
from jax.sharding import Mesh, PartitionSpec as P

NS_ITERS = 8
BLOCK = 1024


def matmul(left, right):
    return jnp.dot(left, right, precision=lax.Precision.HIGHEST, preferred_element_type=jnp.float32)


def inner_rows(left, right):
    return lax.dot_general(
        left,
        right,
        (((0,), (0,)), ((), ())),
        precision=lax.Precision.HIGHEST,
        preferred_element_type=jnp.float32,
    )


def root_pair(matrix):
    order = matrix.shape[0]
    ident = jnp.eye(order, dtype=jnp.float32)
    scale = jnp.trace(matrix)
    ymat = matrix / scale
    zmat = ident
    for step in range(NS_ITERS):
        weight = 1.5 * ident - 0.5 * matmul(zmat, ymat)
        ymat, zmat = (matmul(ymat, weight), matmul(weight, zmat))
    return (jnp.sqrt(scale) * ymat, zmat / jnp.sqrt(scale))


def finish(gram, ritz):
    rank = gram.shape[0]
    ident = jnp.eye(rank, dtype=jnp.float32)
    unused, cinv = root_pair(gram)
    hmat = matmul(matmul(cinv, ritz), cinv)
    eps = 0.1 * jnp.trace(hmat) / rank
    root, rinv = root_pair(hmat + eps * ident)
    return (cinv, root, jnp.sqrt(eps) * rinv - ident)


def exchange(parts, axes):
    return lax.all_to_all(parts, axes, split_axis=0, concat_axis=0, tiled=True)


def gather(block, axes, size):
    return exchange(jnp.broadcast_to(block[None], (size,) + block.shape), axes)


def make_per_device(sizes):
    nz, ny, nx, nc = sizes

    def per_device(inputs, out_grads, sketch):
        whole = gather(inputs, ("x", "core"), nx * nc)
        part = lax.dot_general(
            whole, out_grads, (((1,), (0,)), ((), ())), preferred_element_type=jnp.float32
        ).reshape(BLOCK, BLOCK)
        rows_y = lax.psum_scatter(part, "y", scatter_dimension=0, tiled=True)
        few = rows_y.shape[0] // nz
        rows = jnp.sum(exchange(rows_y.reshape(nz, few, BLOCK), "z"), axis=0)
        slab = gather(rows, "z", nz).reshape(nz * few, BLOCK)
        grad = lax.all_gather(slab, "y", axis=0, tiled=True)

        own = sketch[0]
        sk = gather(own, "y", ny).reshape(-1, own.shape[1])
        sk = gather(sk, "z", nz).reshape(-1, own.shape[1])

        place = lax.axis_index("z") * ny + lax.axis_index("y")
        width = BLOCK // (nz * ny)
        power = 0.95 * matmul(sk, inner_rows(sk, sk)) + matmul(grad, inner_rows(grad, sk))
        gram = inner_rows(power, power)
        spow = inner_rows(sk, power)
        gpow = inner_rows(grad, power)
        ritz = 0.95 * inner_rows(spow, spow) + inner_rows(gpow, gpow)
        cinv, root, middle = finish(gram, ritz)
        basis = matmul(power, cinv)
        fresh = matmul(lax.dynamic_slice_in_dim(basis, place * width, width, 0), root)
        cols = lax.dynamic_slice_in_dim(grad, place * width, width, 1)
        coef = inner_rows(basis, cols)
        update = cols + matmul(basis, matmul(middle, coef))
        return (update[None], fresh[None])

    return per_device


def solution(mesh):
    sizes = (8, 8, 4, 2)
    fine = Mesh(mesh.devices.reshape(sizes), ("z", "y", "x", "core"))
    dp, mp = ("z", "y"), ("x", "core")
    in_specs = (P(dp, mp), P(dp, mp), P(mp, dp, None))
    out_specs = (P(mp, None, dp), P(mp, dp, None))
    return jax.shard_map(
        make_per_device(sizes), mesh=fine, in_specs=in_specs, out_specs=out_specs, check_vma=False
    )
```

```python
import jax
import jax.numpy as jnp
from jax import lax
from jax.experimental import pallas as pl
from jax.experimental.pallas import tpu as pltpu
from jax.sharding import Mesh, PartitionSpec as P

NS_ITERS = 8
BLOCK = 1024
RANK = 256
SIZES = (8, 8, 4, 2)
AXES = ("z", "y", "x", "core")
WIDTH = 16

NN = (((1,), (0,)), ((), ()))
NT = (((1,), (1,)), ((), ()))

THREE = ((0, 1), (1, 0), (0, 0))
FOUR = ((1, 1), (0, 1), (1, 0), (0, 0))
SIX = ((1, 1), (2, 0), (0, 2), (0, 1), (1, 0), (0, 0))


def matmul(left, right):
    return jnp.dot(left, right, precision=lax.Precision.HIGHEST, preferred_element_type=jnp.float32)


def split(value, count):
    pieces = []
    for step in range(count):
        piece = value.astype(jnp.bfloat16)
        pieces.append(piece)
        if step < count - 1:
            value = value - piece.astype(jnp.float32)
    return pieces


def product(left, right, terms, dims=NN):
    total = None
    for i, j in terms:
        term = lax.dot_general(left[i], right[j], dims, preferred_element_type=jnp.float32)
        total = term if total is None else total + term
    return total


def identity():
    rows = lax.broadcasted_iota(jnp.int32, (RANK, RANK), 0)
    cols = lax.broadcasted_iota(jnp.int32, (RANK, RANK), 1)
    return jnp.where(rows == cols, 1.0, 0.0).astype(jnp.float32)


def trace(matrix, ident):
    return jnp.sum(matrix * ident, keepdims=True)


def inverse_root(matrix, ident):
    scale = trace(matrix, ident)
    tmat = matrix * (1.0 / scale)
    zmat = 1.5 * ident - 0.5 * tmat
    for step in range(1, NS_ITERS):
        tsp = split(tmat, 2)
        square = product(tsp, tsp, FOUR)
        cube = product(split(square, 2), tsp, FOUR)
        tmat = 2.25 * tmat - 1.5 * square + 0.25 * cube
        zmat = 1.5 * zmat - 0.5 * product(split(zmat, 2), split(tmat, 2), THREE)
    return zmat * lax.rsqrt(scale)


def full_product(left, right, dims=NN):
    return product(split(left, 3), split(right, 3), SIX, dims)


def finish_kernel(place_ref, grad_ref, skt_ref, base_ref, upd_ref, fresh_ref, high_ref, low_ref, pick_ref, rows_ref, all_ref):
    for part in range(4):
        band = pl.ds(part * 256, 256)
        high, low = split(grad_ref[band, :], 2)
        high_ref[band, :] = high
        low_ref[band, :] = low
    block = pl.ds(pl.multiple_of(place_ref[0] * 128, 128), 128)
    inner = pl.ds(pl.multiple_of(place_ref[1] * WIDTH, WIDTH), WIDTH)
    moved = pl.ds(pl.multiple_of(place_ref[2] * 128, 128), 128)
    pick_ref[...] = grad_ref[:, block].T
    grad = (high_ref[...], low_ref[...])
    skt = skt_ref[...]
    wt = product(split(skt, 2), grad, THREE)
    power = base_ref[...] + product(split(wt, 2), grad, THREE, NT)
    psp = split(power, 3)
    gpow = product(psp, grad, THREE)
    ident = identity()
    gram = product(psp, psp, SIX, NT)
    spow = product(psp, split(skt, 3), SIX, NT)
    ritz = 0.95 * full_product(spow, spow, NT) + full_product(gpow, gpow, NT)
    cinv = inverse_root(gram, ident)
    csp = split(cinv, 3)
    hmat = product(split(product(csp, split(ritz, 3), SIX), 3), csp, SIX)
    eps = trace(hmat, ident) * (0.1 / RANK)
    hdamp = hmat + eps * ident
    rinv = inverse_root(hdamp, ident)
    root = full_product(hdamp, rinv)
    middle = jnp.sqrt(eps) * rinv - ident
    basis = product(csp, psp, SIX)
    bsp = split(basis, 3)
    cols = pick_ref[inner, :]
    coef = product(split(cols, 3), bsp, SIX, NT)
    upd_ref[...] = cols + product(split(full_product(coef, middle, NT), 3), bsp, SIX)
    all_ref[...] = basis
    rows_ref[...] = all_ref[:, moved].T
    fresh_ref[...] = full_product(rows_ref[inner, :], root)


def finish(place, grad, skt, base):
    whole = pl.BlockSpec(memory_space=pltpu.VMEM)
    return pl.pallas_call(
        finish_kernel,
        out_shape=(
            jax.ShapeDtypeStruct((WIDTH, BLOCK), jnp.float32),
            jax.ShapeDtypeStruct((WIDTH, RANK), jnp.float32),
        ),
        in_specs=[pl.BlockSpec(memory_space=pltpu.SMEM), whole, whole, whole],
        out_specs=(whole, whole),
        scratch_shapes=[
            pltpu.VMEM((BLOCK, BLOCK), jnp.bfloat16),
            pltpu.VMEM((BLOCK, BLOCK), jnp.bfloat16),
            pltpu.VMEM((128, BLOCK), jnp.float32),
            pltpu.VMEM((128, RANK), jnp.float32),
            pltpu.VMEM((RANK, BLOCK), jnp.float32),
        ],
        compiler_params=pltpu.CompilerParams(vmem_limit_bytes=40 * 1024 * 1024),
    )(place, grad, skt, base)


def groups(first):
    sets = []
    for x in range(SIZES[2]):
        for other in range(8):
            for core in range(2):
                along_y = (core == 0) == first
                sets.append([
                    (((other * 8 + i) if along_y else (i * 8 + other)) * SIZES[2] + x) * 2 + core
                    for i in range(8)
                ])
    return sets


def exchange(parts, axes, sets=None):
    return lax.all_to_all(
        parts, axes, split_axis=0, concat_axis=0, tiled=True, axis_index_groups=sets
    )


def gather(block, axes, size, sets=None):
    return exchange(jnp.broadcast_to(block[None], (size,) + block.shape), axes, sets)


def per_device(inputs, out_grads, sketch):
    near = gather(inputs, "x", SIZES[2])
    far = lax.ppermute(near, "core", [(0, 1), (1, 0)])
    core = lax.axis_index("core")
    part = lax.dot_general(
        jnp.concatenate([near, far]),
        out_grads,
        (((1,), (0,)), ((), ())),
        preferred_element_type=jnp.float32,
    ).reshape(BLOCK, BLOCK)
    one, two = groups(True), groups(False)
    band = lax.psum_scatter(part, AXES, scatter_dimension=0, tiled=True, axis_index_groups=one)
    own_sk = gather(sketch[0], "y", 8).reshape(-1, RANK)
    own_sk, band = lax.optimization_barrier((own_sk, band))
    rows = jnp.sum(exchange(band.reshape(8, WIDTH, BLOCK), AXES, two), axis=0)
    slab = gather(rows, AXES, 8, two).reshape(8 * WIDTH, BLOCK)
    grad = lax.all_gather(slab, AXES, axis=0, tiled=True, axis_index_groups=one)
    sk = gather(own_sk, "z", 8).reshape(4, 2, 128, RANK).swapaxes(0, 1)
    sk = jnp.where(core == 0, sk, sk[::-1]).reshape(BLOCK, RANK)
    skt = sk.T
    base = 0.95 * matmul(matmul(skt, sk), skt)
    z, y = lax.axis_index("z"), lax.axis_index("y")
    places = jnp.stack([z, y, (z % 2 + core) % 2 * 4 + z // 2])
    update, fresh = finish(places.astype(jnp.int32), grad, skt, base)
    update = update.reshape(WIDTH, 2, 4, 128)
    update = jnp.where(core == 0, update, update[:, ::-1])
    return (update.transpose(2, 1, 3, 0).reshape(1, BLOCK, WIDTH), fresh[None])


def solution(mesh):
    fine = Mesh(mesh.devices.reshape(SIZES), AXES)
    dp, mp = AXES[:2], AXES[2:]
    in_specs = (P(dp, mp), P(dp, mp), P(mp, dp, None))
    out_specs = (P(mp, None, dp), P(mp, dp, None))
    return jax.shard_map(
        per_device, mesh=fine, in_specs=in_specs, out_specs=out_specs, check_vma=False
    )
```

```python
import jax
import jax.numpy as jnp
from jax import lax
from jax.experimental import pallas as pl
from jax.experimental.pallas import tpu as pltpu
from jax.sharding import Mesh, PartitionSpec as P

NS_ITERS = 8
BLOCK = 1024
RANK = 256
SIZES = (8, 8, 4, 2)
AXES = ("z", "y", "x", "core")
WIDTH = 16
PARTS = 4
BAND = BLOCK // PARTS

NN = (((1,), (0,)), ((), ()))
NT = (((1,), (1,)), ((), ()))

THREE = ((0, 1), (1, 0), (0, 0))
SIX = ((1, 1), (2, 0), (0, 2), (0, 1), (1, 0), (0, 0))


def split(value, count):
    pieces = []
    for step in range(count):
        piece = value.astype(jnp.bfloat16)
        pieces.append(piece)
        if step < count - 1:
            value = value - piece.astype(jnp.float32)
    return pieces


def product(left, right, terms, dims=NN):
    total = None
    for i, j in terms:
        term = lax.dot_general(left[i], right[j], dims, preferred_element_type=jnp.float32)
        total = term if total is None else total + term
    return total


def identity():
    rows = lax.broadcasted_iota(jnp.int32, (RANK, RANK), 0)
    cols = lax.broadcasted_iota(jnp.int32, (RANK, RANK), 1)
    return jnp.where(rows == cols, 1.0, 0.0).astype(jnp.float32)


def trace(matrix, ident):
    return jnp.sum(matrix * ident, keepdims=True)


def own_product(value):
    one, two, three = split(value, 3)
    cross = lax.dot_general(
        jnp.concatenate([one, one], axis=1),
        jnp.concatenate([three, two], axis=1),
        NT,
        preferred_element_type=jnp.float32,
    )
    return (cross + cross.T) + product((one, two), (one, two), ((1, 1), (0, 0)), NT)


def inverse_root(matrix, ident):
    scale = trace(matrix, ident)
    tmat = matrix * (1.0 / scale)
    zmat = 1.5 * ident - 0.5 * tmat
    for step in range(1, NS_ITERS):
        tsp = split(tmat, 2)
        square = product(tsp, tsp, THREE)
        cube = product(split(square, 2), tsp, THREE)
        tmat = 2.25 * tmat - 1.5 * square + 0.25 * cube
        zmat = 1.5 * zmat - 0.5 * product(split(zmat, 2), split(tmat, 2), THREE)
    return zmat * lax.rsqrt(scale)


def full_product(left, right):
    return product(split(left, 3), split(right, 3), SIX)


def finish_kernel(
    place_ref, both_ref, upd_ref, fresh_ref,
    wide_ref, high_ref, low_ref, all_ref, pow_ref, pick_ref, rows_ref, sems,
):
    copies = []
    for part in range(PARTS):
        band = pl.ds(part * BAND, BAND)
        copies.append(pltpu.make_async_copy(both_ref.at[band, :], wide_ref.at[band, :], sems.at[part]))
        copies[-1].start()
    wt = None
    for part in range(PARTS):
        copies[part].wait()
        band = pl.ds(part * BAND, BAND)
        high, low = split(wide_ref[band, :], 2)
        high_ref[band, :] = high
        low_ref[band, :] = low
        skt = wide_ref[band, BLOCK:].T
        term = product(split(skt, 2), (high, low), THREE)
        wt = term if wt is None else wt + term
    block = pl.ds(pl.multiple_of(place_ref[0] * 128, 128), 128)
    inner = pl.ds(pl.multiple_of(place_ref[1] * WIDTH, WIDTH), WIDTH)
    moved = pl.ds(pl.multiple_of(place_ref[2] * 128, 128), 128)
    lane = lax.broadcasted_iota(jnp.int32, (1, BLOCK + RANK), 1)

    both = (high_ref[...], low_ref[...])
    power = product(split(wt * jnp.where(lane < BLOCK, 1.0, 0.95), 2), both, THREE, NT)
    ident = identity()
    psp = split(power, 3)
    gram = own_product(power)
    gpow = product(psp, both, THREE)
    ritz = own_product(gpow * jnp.where(lane < BLOCK, 1.0, 0.95 ** 0.5))
    cinv = inverse_root(gram, ident)
    csp = split(cinv, 3)
    pick_ref[...] = wide_ref[:, block].T
    cols = pick_ref[inner, :]
    pow_ref[...] = power
    rows_ref[...] = pow_ref[:, moved].T
    prow = rows_ref[inner, :]
    all_ref[...] = gpow
    rows_ref[...] = all_ref[:, block].T
    gcol = rows_ref[inner, :]
    pair = product(split(jnp.concatenate([prow, gcol], axis=0), 3), csp, SIX)
    hmat = product(split(product(csp, split(ritz, 3), SIX), 3), csp, SIX)
    eps = trace(hmat, ident) * (0.1 / RANK)
    hdamp = hmat + eps * ident
    lead = full_product(pair[:WIDTH], hdamp)
    rinv = inverse_root(hdamp, ident)
    last = full_product(jnp.concatenate([lead, pair[WIDTH:]], axis=0), rinv)
    fresh_ref[...] = last[:WIDTH]
    middle = jnp.sqrt(eps) * last[WIDTH:] - pair[WIDTH:]
    coef = product(split(middle, 3), csp, SIX)
    upd_ref[...] = cols + product(split(coef, 3), psp, SIX)


def finish(places, both):
    whole = pl.BlockSpec(memory_space=pltpu.VMEM)
    return pl.pallas_call(
        finish_kernel,
        out_shape=(
            jax.ShapeDtypeStruct((WIDTH, BLOCK), jnp.float32),
            jax.ShapeDtypeStruct((WIDTH, RANK), jnp.float32),
        ),
        in_specs=[pl.BlockSpec(memory_space=pltpu.SMEM), pl.BlockSpec(memory_space=pltpu.HBM)],
        out_specs=(whole, whole),
        scratch_shapes=[
            pltpu.VMEM((BLOCK, BLOCK + RANK), jnp.float32),
            pltpu.VMEM((BLOCK, BLOCK + RANK), jnp.bfloat16),
            pltpu.VMEM((BLOCK, BLOCK + RANK), jnp.bfloat16),
            pltpu.VMEM((RANK, BLOCK + RANK), jnp.float32),
            pltpu.VMEM((RANK, BLOCK), jnp.float32),
            pltpu.VMEM((128, BLOCK), jnp.float32),
            pltpu.VMEM((128, RANK), jnp.float32),
            pltpu.SemaphoreType.DMA((PARTS,)),
        ],
        compiler_params=pltpu.CompilerParams(vmem_limit_bytes=48 * 1024 * 1024),
    )(places, both)


def groups(first):
    sets = []
    for x in range(SIZES[2]):
        for other in range(8):
            for core in range(2):
                along_y = (core == 0) == first
                sets.append([
                    (((other * 8 + i) if along_y else (i * 8 + other)) * SIZES[2] + x) * 2 + core
                    for i in range(8)
                ])
    return sets


def sketch_moves():
    nz, ny, nx, nc = SIZES
    moves = []
    for z in range(nz):
        for y in range(ny):
            for x in range(nx):
                for core in range(nc):
                    position, inner = (y, z) if core == 0 else (z, y)
                    natural = position % 4 * 2 + (position // 4 + core) % 2
                    source = ((natural * ny + inner) * nx + x) * nc + core
                    moves.append((source, ((z * ny + y) * nx + x) * nc + core))
    return moves


def exchange(parts, axes, sets=None):
    return lax.all_to_all(
        parts, axes, split_axis=0, concat_axis=0, tiled=True, axis_index_groups=sets
    )


def gather(block, axes, size, sets=None):
    return exchange(jnp.broadcast_to(block[None], (size,) + block.shape), axes, sets)


def per_device(inputs, out_grads, sketch):
    near = gather(inputs, "x", SIZES[2])
    far = lax.ppermute(near, "core", [(0, 1), (1, 0)])
    core = lax.axis_index("core")
    part = lax.dot_general(
        jnp.concatenate([near, far]),
        out_grads,
        (((1,), (0,)), ((), ())),
        preferred_element_type=jnp.float32,
    ).reshape(BLOCK, BLOCK)
    part, own_sk = lax.optimization_barrier((part, sketch[0]))
    one, two = groups(True), groups(False)
    band = lax.psum_scatter(part, AXES, scatter_dimension=0, tiled=True, axis_index_groups=one)
    own_sk = lax.ppermute(own_sk, AXES, sketch_moves())
    rows = jnp.sum(exchange(band.reshape(8, WIDTH, BLOCK), AXES, two), axis=0)
    rows = jnp.concatenate([rows, own_sk], axis=1)
    slab = gather(rows, AXES, 8, two).reshape(8 * WIDTH, BLOCK + RANK)
    both = lax.all_gather(slab, AXES, axis=0, tiled=True, axis_index_groups=one)
    z, y = lax.axis_index("z"), lax.axis_index("y")
    places = jnp.stack([z, y, (z % 2 + core) % 2 * 4 + z // 2])
    update, fresh = finish(places.astype(jnp.int32), both)
    update = update.reshape(WIDTH, 2, 4, 128)
    update = jnp.where(core == 0, update, update[:, ::-1])
    return (update.transpose(2, 1, 3, 0).reshape(1, BLOCK, WIDTH), fresh[None])


def solution(mesh):
    fine = Mesh(mesh.devices.reshape(SIZES), AXES)
    dp, mp = AXES[:2], AXES[2:]
    in_specs = (P(dp, mp), P(dp, mp), P(mp, dp, None))
    out_specs = (P(mp, None, dp), P(mp, dp, None))
    return jax.shard_map(
        per_device, mesh=fine, in_specs=in_specs, out_specs=out_specs, check_vma=False
    )
```

```python
import jax
import jax.numpy as jnp
from jax import lax
from jax.experimental import pallas as pl
from jax.experimental.pallas import tpu as pltpu
from jax.sharding import Mesh, PartitionSpec as P

NS_ITERS = 8
BLOCK = 1024
RANK = 256
SIZES = (8, 8, 4, 2)
AXES = ("z", "y", "x", "core")
WIDTH = 16
PARTS = 2
BAND = BLOCK // PARTS

NN = (((1,), (0,)), ((), ()))
NT = (((1,), (1,)), ((), ()))

THREE = ((0, 1), (1, 0), (0, 0))
SIX = ((1, 1), (2, 0), (0, 2), (0, 1), (1, 0), (0, 0))


def split(value, count):
    pieces = []
    for step in range(count):
        piece = value.astype(jnp.bfloat16)
        pieces.append(piece)
        if step < count - 1:
            value = value - piece.astype(jnp.float32)
    return pieces


def product(left, right, terms, dims=NN):
    total = None
    for i, j in terms:
        term = lax.dot_general(left[i], right[j], dims, preferred_element_type=jnp.float32)
        total = term if total is None else total + term
    return total


def identity():
    rows = lax.broadcasted_iota(jnp.int32, (RANK, RANK), 0)
    cols = lax.broadcasted_iota(jnp.int32, (RANK, RANK), 1)
    return jnp.where(rows == cols, 1.0, 0.0).astype(jnp.float32)


def trace(matrix, ident):
    return jnp.sum(matrix * ident, keepdims=True)


def own_product(value):
    one, two, three = split(value, 3)
    cross = lax.dot_general(
        jnp.concatenate([one, one], axis=1),
        jnp.concatenate([three, two], axis=1),
        NT,
        preferred_element_type=jnp.float32,
    )
    return (cross + cross.T) + product((one, two), (one, two), ((1, 1), (0, 0)), NT)


def inverse_root(matrix, ident, beside=lambda step: None):
    scale = trace(matrix, ident)
    tmat = matrix * (1.0 / scale)
    zmat = 1.5 * ident - 0.5 * tmat
    for step in range(1, NS_ITERS):
        tsp = split(tmat, 2)
        square = product(tsp, tsp, THREE)
        beside(step)
        cube = product(split(square, 2), tsp, THREE)
        tmat = 2.25 * tmat - 1.5 * square + 0.25 * cube
        zmat = 1.5 * zmat - 0.5 * product(split(zmat, 2), split(tmat, 2), THREE)
    return zmat * lax.rsqrt(scale)


def full_product(left, right):
    return product(split(left, 3), split(right, 3), SIX)


def finish_kernel(
    place_ref, both_ref, upd_ref, fresh_ref,
    wide_ref, high_ref, low_ref, all_ref, pow_ref, pick_ref, rows_ref, sems,
):
    copies = []
    for part in range(PARTS):
        band = pl.ds(part * BAND, BAND)
        copies.append(pltpu.make_async_copy(both_ref.at[band, :], wide_ref.at[band, :], sems.at[part]))
        copies[-1].start()
    wt = None
    for part in range(PARTS):
        copies[part].wait()
        band = pl.ds(part * BAND, BAND)
        high, low = split(wide_ref[band, :], 2)
        high_ref[band, :] = high
        low_ref[band, :] = low
        skt = wide_ref[band, BLOCK:].T
        term = product(split(skt, 2), (high, low), THREE)
        wt = term if wt is None else wt + term
    block = pl.ds(pl.multiple_of(place_ref[0] * 128, 128), 128)
    inner = pl.ds(pl.multiple_of(place_ref[1] * WIDTH, WIDTH), WIDTH)
    moved = pl.ds(pl.multiple_of(place_ref[2] * 128, 128), 128)

    both = (high_ref[...], low_ref[...])
    lane = lax.broadcasted_iota(jnp.int32, (1, BLOCK + RANK), 1)
    weight = jnp.where(lane < BLOCK, 1.0, 0.95)
    power = product(split(wt * weight, 2), both, THREE, NT)
    ident = identity()
    psp = split(power, 3)
    gram = own_product(power)
    ritz = []

    def beside(step):
        if step <= (BLOCK + RANK) // 256:
            part = pl.ds((step - 1) * 256, 256)
            gpow = product(psp[:2], (high_ref[:, part], low_ref[:, part]), THREE)
            all_ref[:, part] = gpow
            ritz.append(gpow if step <= BLOCK // 256 else gpow * 0.95 ** 0.5)

    cinv = inverse_root(gram, ident, beside)
    ritz = own_product(jnp.concatenate(ritz, axis=1))
    csp = split(cinv, 3)
    pick_ref[...] = wide_ref[:, block].T
    cols = pick_ref[inner, :]
    pow_ref[...] = power
    rows_ref[...] = pow_ref[:, moved].T
    prow = rows_ref[inner, :]
    rows_ref[...] = all_ref[:, block].T
    gcol = rows_ref[inner, :]
    pair = product(split(jnp.concatenate([prow, gcol], axis=0), 3), csp, SIX)
    hmat = product(split(product(csp, split(ritz, 3), SIX), 3), csp, SIX)
    eps = trace(hmat, ident) * (0.1 / RANK)
    hdamp = hmat + eps * ident
    lead = full_product(pair[:WIDTH], hdamp)
    rinv = inverse_root(hdamp, ident)
    last = full_product(jnp.concatenate([lead, pair[WIDTH:]], axis=0), rinv)
    fresh_ref[...] = last[:WIDTH]
    middle = jnp.sqrt(eps) * last[WIDTH:] - pair[WIDTH:]
    coef = product(split(middle, 3), csp, SIX)
    update = cols + product(split(coef, 3), psp, SIX)
    for natural in range(8):
        ahead, across = natural // 2, natural % 2
        blocks = [update[:, (4 * side + ahead) * 128:(4 * side + ahead + 1) * 128] for side in (0, 1)]
        upd_ref[:, natural * 128:(natural + 1) * 128] = jnp.where(
            place_ref[3] == 0, blocks[across], blocks[1 - across]
        )


def finish(places, both):
    whole = pl.BlockSpec(memory_space=pltpu.VMEM)
    return pl.pallas_call(
        finish_kernel,
        out_shape=(
            jax.ShapeDtypeStruct((WIDTH, BLOCK), jnp.float32),
            jax.ShapeDtypeStruct((WIDTH, RANK), jnp.float32),
        ),
        in_specs=[pl.BlockSpec(memory_space=pltpu.SMEM), pl.BlockSpec(memory_space=pltpu.HBM)],
        out_specs=(whole, whole),
        scratch_shapes=[
            pltpu.VMEM((BLOCK, BLOCK + RANK), jnp.float32),
            pltpu.VMEM((BLOCK, BLOCK + RANK), jnp.bfloat16),
            pltpu.VMEM((BLOCK, BLOCK + RANK), jnp.bfloat16),
            pltpu.VMEM((RANK, BLOCK + RANK), jnp.float32),
            pltpu.VMEM((RANK, BLOCK), jnp.float32),
            pltpu.VMEM((128, BLOCK), jnp.float32),
            pltpu.VMEM((128, RANK), jnp.float32),
            pltpu.SemaphoreType.DMA((PARTS,)),
        ],
        compiler_params=pltpu.CompilerParams(vmem_limit_bytes=60 * 1024 * 1024),
    )(places, both)


def groups(first):
    sets = []
    for x in range(SIZES[2]):
        for other in range(8):
            for core in range(2):
                along_y = (core == 0) == first
                sets.append([
                    (((other * 8 + i) if along_y else (i * 8 + other)) * SIZES[2] + x) * 2 + core
                    for i in range(8)
                ])
    return sets


def sketch_moves():
    nz, ny, nx, nc = SIZES
    moves = []
    for z in range(nz):
        for y in range(ny):
            for x in range(nx):
                for core in range(nc):
                    position, inner = (y, z) if core == 0 else (z, y)
                    natural = position % 4 * 2 + (position // 4 + core) % 2
                    source = ((natural * ny + inner) * nx + x) * nc + core
                    moves.append((source, ((z * ny + y) * nx + x) * nc + core))
    return moves


def exchange(parts, axes, sets=None):
    return lax.all_to_all(
        parts, axes, split_axis=0, concat_axis=0, tiled=True, axis_index_groups=sets
    )


def gather(block, axes, size, sets=None):
    return exchange(jnp.broadcast_to(block[None], (size,) + block.shape), axes, sets)


def per_device(inputs, out_grads, sketch):
    near = gather(inputs, "x", SIZES[2])
    far = lax.ppermute(near, "core", [(0, 1), (1, 0)])
    core = lax.axis_index("core")
    part = lax.dot_general(
        jnp.concatenate([near, far]),
        out_grads,
        (((1,), (0,)), ((), ())),
        preferred_element_type=jnp.float32,
    ).reshape(BLOCK, BLOCK)
    part, own_sk = lax.optimization_barrier((part, sketch[0]))
    one, two = groups(True), groups(False)
    band = lax.psum_scatter(part, AXES, scatter_dimension=0, tiled=True, axis_index_groups=one)
    own_sk = lax.ppermute(own_sk, AXES, sketch_moves())
    own_sk, band = lax.optimization_barrier((own_sk, band))
    rows = jnp.sum(exchange(band.reshape(8, WIDTH, BLOCK), AXES, two), axis=0)
    rows = jnp.concatenate([rows, own_sk], axis=1)
    slab = gather(rows, AXES, 8, two).reshape(8 * WIDTH, BLOCK + RANK)
    both = lax.all_gather(slab, AXES, axis=0, tiled=True, axis_index_groups=one)
    z, y = lax.axis_index("z"), lax.axis_index("y")
    places = jnp.stack([z, y, (z % 2 + core) % 2 * 4 + z // 2, core])
    update, fresh = finish(places.astype(jnp.int32), both)
    return (update.T[None], fresh[None])


def solution(mesh):
    fine = Mesh(mesh.devices.reshape(SIZES), AXES)
    dp, mp = AXES[:2], AXES[2:]
    in_specs = (P(dp, mp), P(dp, mp), P(mp, dp, None))
    out_specs = (P(mp, None, dp), P(mp, dp, None))
    return jax.shard_map(
        per_device, mesh=fine, in_specs=in_specs, out_specs=out_specs, check_vma=False
    )
```

```python
import jax
import jax.numpy as jnp
from jax import lax
from jax.experimental import pallas as pl
from jax.experimental.pallas import tpu as pltpu
from jax.sharding import Mesh, PartitionSpec as P

NS_ITERS = 8
BLOCK = 1024
RANK = 256
SIZES = (8, 8, 4, 2)
AXES = ("z", "y", "x", "core")
WIDTH = 16
PARTS = 2
BAND = BLOCK // PARTS

NN = (((1,), (0,)), ((), ()))
NT = (((1,), (1,)), ((), ()))

THREE = ((0, 1), (1, 0), (0, 0))
SIX = ((1, 1), (2, 0), (0, 2), (0, 1), (1, 0), (0, 0))


def matmul(left, right):
    return jnp.dot(left, right, precision=lax.Precision.HIGHEST, preferred_element_type=jnp.float32)


def split(value, count):
    pieces = []
    for step in range(count):
        piece = value.astype(jnp.bfloat16)
        pieces.append(piece)
        if step < count - 1:
            value = value - piece.astype(jnp.float32)
    return pieces


def product(left, right, terms, dims=NN):
    total = None
    for i, j in terms:
        term = lax.dot_general(left[i], right[j], dims, preferred_element_type=jnp.float32)
        total = term if total is None else total + term
    return total


def identity():
    rows = lax.broadcasted_iota(jnp.int32, (RANK, RANK), 0)
    cols = lax.broadcasted_iota(jnp.int32, (RANK, RANK), 1)
    return jnp.where(rows == cols, 1.0, 0.0).astype(jnp.float32)


def trace(matrix, ident):
    return jnp.sum(matrix * ident, keepdims=True)


def own_product(value):
    one, two, three = split(value, 3)
    cross = lax.dot_general(
        jnp.concatenate([one, one], axis=1),
        jnp.concatenate([three, two], axis=1),
        NT,
        preferred_element_type=jnp.float32,
    )
    return (cross + cross.T) + product((one, two), (one, two), ((1, 1), (0, 0)), NT)


def inverse_root(matrix, ident, beside=lambda step: None):
    scale = trace(matrix, ident)
    tmat = matrix * (1.0 / scale)
    zmat = 1.5 * ident - 0.5 * tmat
    for step in range(1, NS_ITERS):
        tsp = split(tmat, 2)
        square = product(tsp, tsp, THREE)
        beside(step)
        cube = product(split(square, 2), tsp, THREE)
        tmat = 2.25 * tmat - 1.5 * square + 0.25 * cube
        zmat = 1.5 * zmat - 0.5 * product(split(zmat, 2), split(tmat, 2), THREE)
    return zmat * lax.rsqrt(scale)


def full_product(left, right):
    return product(split(left, 3), split(right, 3), SIX)


def finish_kernel(
    place_ref, grad_ref, skt_ref, base_ref, upd_ref, fresh_ref,
    wide_ref, high_ref, low_ref, all_ref, pow_ref, pick_ref, rows_ref, sems,
):
    copies = []
    for part in range(PARTS):
        band = pl.ds(part * BAND, BAND)
        copies.append(pltpu.make_async_copy(grad_ref.at[band, :], wide_ref.at[band, :], sems.at[part]))
        copies[-1].start()
    ssp = split(skt_ref[...], 2)
    wt = None
    for part in range(PARTS):
        copies[part].wait()
        band = pl.ds(part * BAND, BAND)
        high, low = split(wide_ref[band, :], 2)
        high_ref[band, :] = high
        low_ref[band, :] = low
        own = [piece[:, part * BAND:(part + 1) * BAND] for piece in ssp]
        term = product(own, (high, low), THREE)
        wt = term if wt is None else wt + term
    block = pl.ds(pl.multiple_of(place_ref[0] * 128, 128), 128)
    inner = pl.ds(pl.multiple_of(place_ref[1] * WIDTH, WIDTH), WIDTH)
    moved = pl.ds(pl.multiple_of(place_ref[2] * 128, 128), 128)

    both = (high_ref[...], low_ref[...])
    power = base_ref[...] + product(split(wt, 2), both, THREE, NT)
    ident = identity()
    psp = split(power, 3)
    gram = own_product(power)
    ritz = []

    def beside(step):
        if step <= BLOCK // 256:
            part = pl.ds((step - 1) * 256, 256)
            gpow = product(psp[:2], (high_ref[:, part], low_ref[:, part]), THREE)
            all_ref[:, part] = gpow
            ritz.append(gpow)
        elif step == BLOCK // 256 + 1:
            ritz.append(product(psp[:2], ssp, THREE, NT) * 0.95 ** 0.5)

    cinv = inverse_root(gram, ident, beside)
    ritz = own_product(jnp.concatenate(ritz, axis=1))
    csp = split(cinv, 3)
    pick_ref[...] = wide_ref[:, block].T
    cols = pick_ref[inner, :]
    pow_ref[...] = power
    rows_ref[...] = pow_ref[:, moved].T
    prow = rows_ref[inner, :]
    rows_ref[...] = all_ref[:, block].T
    gcol = rows_ref[inner, :]
    pair = product(split(jnp.concatenate([prow, gcol], axis=0), 3), csp, SIX)
    hmat = product(split(product(csp, split(ritz, 3), SIX), 3), csp, SIX)
    eps = trace(hmat, ident) * (0.1 / RANK)
    hdamp = hmat + eps * ident
    lead = full_product(pair[:WIDTH], hdamp)
    rinv = inverse_root(hdamp, ident)
    last = full_product(jnp.concatenate([lead, pair[WIDTH:]], axis=0), rinv)
    fresh_ref[...] = last[:WIDTH]
    middle = jnp.sqrt(eps) * last[WIDTH:] - pair[WIDTH:]
    coef = product(split(middle, 3), csp, SIX)
    update = cols + product(split(coef, 3), psp, SIX)
    for natural in range(8):
        ahead, across = natural // 2, natural % 2
        blocks = [update[:, (4 * side + ahead) * 128:(4 * side + ahead + 1) * 128] for side in (0, 1)]
        upd_ref[:, natural * 128:(natural + 1) * 128] = jnp.where(
            place_ref[3] == 0, blocks[across], blocks[1 - across]
        )


def finish(places, grad, skt, base):
    whole = pl.BlockSpec(memory_space=pltpu.VMEM)
    return pl.pallas_call(
        finish_kernel,
        out_shape=(
            jax.ShapeDtypeStruct((WIDTH, BLOCK), jnp.float32),
            jax.ShapeDtypeStruct((WIDTH, RANK), jnp.float32),
        ),
        in_specs=[
            pl.BlockSpec(memory_space=pltpu.SMEM),
            pl.BlockSpec(memory_space=pltpu.HBM),
            whole,
            whole,
        ],
        out_specs=(whole, whole),
        scratch_shapes=[
            pltpu.VMEM((BLOCK, BLOCK), jnp.float32),
            pltpu.VMEM((BLOCK, BLOCK), jnp.bfloat16),
            pltpu.VMEM((BLOCK, BLOCK), jnp.bfloat16),
            pltpu.VMEM((RANK, BLOCK), jnp.float32),
            pltpu.VMEM((RANK, BLOCK), jnp.float32),
            pltpu.VMEM((128, BLOCK), jnp.float32),
            pltpu.VMEM((128, RANK), jnp.float32),
            pltpu.SemaphoreType.DMA((PARTS,)),
        ],
        compiler_params=pltpu.CompilerParams(vmem_limit_bytes=57 * 1024 * 1024),
    )(places, grad, skt, base)


def groups(first):
    sets = []
    for x in range(SIZES[2]):
        for other in range(8):
            for core in range(2):
                along_y = (core == 0) == first
                sets.append([
                    (((other * 8 + i) if along_y else (i * 8 + other)) * SIZES[2] + x) * 2 + core
                    for i in range(8)
                ])
    return sets


def exchange(parts, axes, sets=None):
    return lax.all_to_all(
        parts, axes, split_axis=0, concat_axis=0, tiled=True, axis_index_groups=sets
    )


def gather(block, axes, size, sets=None):
    return exchange(jnp.broadcast_to(block[None], (size,) + block.shape), axes, sets)


def per_device(inputs, out_grads, sketch):
    near = gather(inputs, "x", SIZES[2])
    far = lax.ppermute(near, "core", [(0, 1), (1, 0)])
    core = lax.axis_index("core")
    part = lax.dot_general(
        jnp.concatenate([near, far]),
        out_grads,
        (((1,), (0,)), ((), ())),
        preferred_element_type=jnp.float32,
    ).reshape(BLOCK, BLOCK)
    part, own_sk = lax.optimization_barrier((part, sketch[0]))
    one, two = groups(True), groups(False)
    band = lax.psum_scatter(part, AXES, scatter_dimension=0, tiled=True, axis_index_groups=one)
    sk = gather(own_sk, AXES, 8, one).reshape(8 * WIDTH, RANK)
    sk = gather(sk, AXES, 8, two)
    sk, band = lax.optimization_barrier((sk, band))
    rows = jnp.sum(exchange(band.reshape(8, WIDTH, BLOCK), AXES, two), axis=0)
    slab = gather(rows, AXES, 8, two).reshape(8 * WIDTH, BLOCK)
    grad = lax.all_gather(slab, AXES, axis=0, tiled=True, axis_index_groups=one)

    sk = sk.reshape(8, 8, WIDTH, RANK)
    sk = jnp.where(core == 0, sk, sk.swapaxes(0, 1)).reshape(4, 2, 128, RANK).swapaxes(0, 1)
    sk = jnp.where(core == 0, sk, sk[::-1]).reshape(BLOCK, RANK)
    skt = sk.T
    base = 0.95 * matmul(matmul(skt, sk), skt)
    z, y = lax.axis_index("z"), lax.axis_index("y")
    places = jnp.stack([z, y, (z % 2 + core) % 2 * 4 + z // 2, core])
    update, fresh = finish(places.astype(jnp.int32), grad, skt, base)
    return (update.T[None], fresh[None])


def solution(mesh):
    fine = Mesh(mesh.devices.reshape(SIZES), AXES)
    dp, mp = AXES[:2], AXES[2:]
    in_specs = (P(dp, mp), P(dp, mp), P(mp, dp, None))
    out_specs = (P(mp, None, dp), P(mp, dp, None))
    return jax.shard_map(
        per_device, mesh=fine, in_specs=in_specs, out_specs=out_specs, check_vma=False
    )
```

```python
import jax
import jax.numpy as jnp
from jax import lax
from jax.experimental import pallas as pl
from jax.experimental.pallas import tpu as pltpu
from jax.sharding import Mesh, PartitionSpec as P

NS_ITERS = 8
BLOCK = 1024
RANK = 256
SIZES = (8, 8, 4, 2)
AXES = ("z", "y", "x", "core")
WIDTH = 16
PARTS = 2
BAND = BLOCK // PARTS

NN = (((1,), (0,)), ((), ()))
NT = (((1,), (1,)), ((), ()))

THREE = ((0, 1), (1, 0), (0, 0))
SIX = ((1, 1), (2, 0), (0, 2), (0, 1), (1, 0), (0, 0))


def matmul(left, right):
    return jnp.dot(left, right, precision=lax.Precision.HIGHEST, preferred_element_type=jnp.float32)


def split(value, count):
    pieces = []
    for step in range(count):
        piece = value.astype(jnp.bfloat16)
        pieces.append(piece)
        if step < count - 1:
            value = value - piece.astype(jnp.float32)
    return pieces


def product(left, right, terms, dims=NN):
    total = None
    for i, j in terms:
        term = lax.dot_general(left[i], right[j], dims, preferred_element_type=jnp.float32)
        total = term if total is None else total + term
    return total


def identity():
    rows = lax.broadcasted_iota(jnp.int32, (RANK, RANK), 0)
    cols = lax.broadcasted_iota(jnp.int32, (RANK, RANK), 1)
    return jnp.where(rows == cols, 1.0, 0.0).astype(jnp.float32)


def trace(matrix, ident):
    return jnp.sum(matrix * ident, keepdims=True)


def own_product(value):
    one, two, three = split(value, 3)
    cross = lax.dot_general(
        jnp.concatenate([one, one], axis=1),
        jnp.concatenate([three, two], axis=1),
        NT,
        preferred_element_type=jnp.float32,
    )
    return (cross + cross.T) + product((one, two), (one, two), ((1, 1), (0, 0)), NT)


def inverse_root(matrix, ident, beside=lambda step: None):
    scale = trace(matrix, ident)
    tmat = matrix * (1.0 / scale)
    zmat = 1.5 * ident - 0.5 * tmat
    for step in range(1, NS_ITERS):
        tsp = split(tmat, 2)
        square = product(tsp, tsp, THREE)
        beside(step)
        cube = product(split(square, 2), tsp, THREE)
        tmat = 2.25 * tmat - 1.5 * square + 0.25 * cube
        zmat = 1.5 * zmat - 0.5 * product(split(zmat, 2), split(tmat, 2), THREE)
    return zmat * lax.rsqrt(scale)


def few_rows(left, right):
    one, two, three = split(left, 3)
    rows = left.shape[0]
    first = lax.dot_general(
        jnp.concatenate([three, two, one]), right[0], NN, preferred_element_type=jnp.float32
    )
    second = lax.dot_general(
        jnp.concatenate([two, one]), right[1], NN, preferred_element_type=jnp.float32
    )
    third = lax.dot_general(one, right[2], NN, preferred_element_type=jnp.float32)
    low = second[:rows] + third + first[:rows]
    return low + (second[rows:] + first[rows:2 * rows]) + first[2 * rows:]


def finish_kernel(
    place_ref, grad_ref, skt_ref, base_ref, upd_ref, fresh_ref,
    wide_ref, high_ref, low_ref, all_ref, pow_ref, pick_ref, rows_ref, sems,
):
    copies = []
    for part in range(PARTS):
        band = pl.ds(part * BAND, BAND)
        copies.append(pltpu.make_async_copy(grad_ref.at[band, :], wide_ref.at[band, :], sems.at[part]))
        copies[-1].start()
    ssp = split(skt_ref[...], 2)
    wt = None
    for part in range(PARTS):
        copies[part].wait()
        band = pl.ds(part * BAND, BAND)
        high, low = split(wide_ref[band, :], 2)
        high_ref[band, :] = high
        low_ref[band, :] = low
        own = [piece[:, part * BAND:(part + 1) * BAND] for piece in ssp]
        term = product(own, (high, low), THREE)
        wt = term if wt is None else wt + term
    block = pl.ds(pl.multiple_of(place_ref[0] * 128, 128), 128)
    inner = pl.ds(pl.multiple_of(place_ref[1] * WIDTH, WIDTH), WIDTH)
    moved = pl.ds(pl.multiple_of(place_ref[2] * 128, 128), 128)

    both = (high_ref[...], low_ref[...])
    power = base_ref[...] + product(split(wt, 2), both, THREE, NT)
    ident = identity()
    psp = split(power, 3)
    gram = own_product(power)
    ritz = []

    def beside(step):
        if step <= BLOCK // 256:
            part = pl.ds((step - 1) * 256, 256)
            gpow = product(psp[:2], (high_ref[:, part], low_ref[:, part]), THREE)
            all_ref[:, part] = gpow
            ritz.append(gpow)
        elif step == BLOCK // 256 + 1:
            ritz.append(product(psp[:2], ssp, THREE, NT) * 0.95 ** 0.5)

    cinv = inverse_root(gram, ident, beside)
    ritz = own_product(jnp.concatenate(ritz, axis=1))
    csp = split(cinv, 3)
    pick_ref[...] = wide_ref[:, block].T
    cols = pick_ref[inner, :]
    pow_ref[...] = power
    rows_ref[...] = pow_ref[:, moved].T
    prow = rows_ref[inner, :]
    rows_ref[...] = all_ref[:, block].T
    gcol = rows_ref[inner, :]
    hmat = product(split(product(csp, split(ritz, 3), SIX), 3), csp, SIX)
    eps = trace(hmat, ident) * (0.1 / RANK)
    hdamp = hmat + eps * ident
    held = []

    def late(step):
        if step == 1:
            held.append(few_rows(jnp.concatenate([prow, gcol], axis=0), csp))
        if step == 2:
            held.append(few_rows(held[0][:WIDTH], split(hdamp, 3)))

    rinv = inverse_root(hdamp, ident, late)
    pair, lead = held
    last = few_rows(jnp.concatenate([lead, pair[WIDTH:]], axis=0), split(rinv, 3))
    fresh_ref[...] = last[:WIDTH]
    middle = jnp.sqrt(eps) * last[WIDTH:] - pair[WIDTH:]
    coef = few_rows(middle, csp)
    update = cols + few_rows(coef, psp)
    for natural in range(8):
        ahead, across = natural // 2, natural % 2
        blocks = [update[:, (4 * side + ahead) * 128:(4 * side + ahead + 1) * 128] for side in (0, 1)]
        upd_ref[:, natural * 128:(natural + 1) * 128] = jnp.where(
            place_ref[3] == 0, blocks[across], blocks[1 - across]
        )


def finish(places, grad, skt, base):
    whole = pl.BlockSpec(memory_space=pltpu.VMEM)
    return pl.pallas_call(
        finish_kernel,
        out_shape=(
            jax.ShapeDtypeStruct((WIDTH, BLOCK), jnp.float32),
            jax.ShapeDtypeStruct((WIDTH, RANK), jnp.float32),
        ),
        in_specs=[
            pl.BlockSpec(memory_space=pltpu.SMEM),
            pl.BlockSpec(memory_space=pltpu.HBM),
            whole,
            whole,
        ],
        out_specs=(whole, whole),
        scratch_shapes=[
            pltpu.VMEM((BLOCK, BLOCK), jnp.float32),
            pltpu.VMEM((BLOCK, BLOCK), jnp.bfloat16),
            pltpu.VMEM((BLOCK, BLOCK), jnp.bfloat16),
            pltpu.VMEM((RANK, BLOCK), jnp.float32),
            pltpu.VMEM((RANK, BLOCK), jnp.float32),
            pltpu.VMEM((128, BLOCK), jnp.float32),
            pltpu.VMEM((128, RANK), jnp.float32),
            pltpu.SemaphoreType.DMA((PARTS,)),
        ],
        compiler_params=pltpu.CompilerParams(vmem_limit_bytes=57 * 1024 * 1024),
    )(places, grad, skt, base)


def groups(first):
    sets = []
    for x in range(SIZES[2]):
        for other in range(8):
            for core in range(2):
                along_y = (core == 0) == first
                sets.append([
                    (((other * 8 + i) if along_y else (i * 8 + other)) * SIZES[2] + x) * 2 + core
                    for i in range(8)
                ])
    return sets


def exchange(parts, axes, sets=None):
    return lax.all_to_all(
        parts, axes, split_axis=0, concat_axis=0, tiled=True, axis_index_groups=sets
    )


def gather(block, axes, size, sets=None):
    return exchange(jnp.broadcast_to(block[None], (size,) + block.shape), axes, sets)


def per_device(inputs, out_grads, sketch):
    near = gather(inputs, "x", SIZES[2])
    far = lax.ppermute(near, "core", [(0, 1), (1, 0)])
    core = lax.axis_index("core")
    part = lax.dot_general(
        jnp.concatenate([near, far]),
        out_grads,
        (((1,), (0,)), ((), ())),
        preferred_element_type=jnp.float32,
    ).reshape(BLOCK, BLOCK)
    part, own_sk = lax.optimization_barrier((part, sketch[0]))
    one, two = groups(True), groups(False)
    band = lax.psum_scatter(part, AXES, scatter_dimension=0, tiled=True, axis_index_groups=one)
    sk = gather(own_sk, AXES, 8, one).reshape(8 * WIDTH, RANK)
    sk, band = lax.optimization_barrier((sk, band))
    rows = jnp.sum(exchange(band.reshape(8, WIDTH, BLOCK), AXES, two), axis=0)
    slab = gather(rows, AXES, 8, two).reshape(8 * WIDTH, BLOCK)
    grad = lax.all_gather(slab, AXES, axis=0, tiled=True, axis_index_groups=one)

    sk = gather(sk, AXES, 8, two)
    sk = sk.reshape(8, 8, WIDTH, RANK)
    sk = jnp.where(core == 0, sk, sk.swapaxes(0, 1)).reshape(4, 2, 128, RANK).swapaxes(0, 1)
    sk = jnp.where(core == 0, sk, sk[::-1]).reshape(BLOCK, RANK)
    skt = sk.T
    base = 0.95 * matmul(matmul(skt, sk), skt)
    z, y = lax.axis_index("z"), lax.axis_index("y")
    places = jnp.stack([z, y, (z % 2 + core) % 2 * 4 + z // 2, core])
    update, fresh = finish(places.astype(jnp.int32), grad, skt, base)
    return (update.T[None], fresh[None])


def solution(mesh):
    fine = Mesh(mesh.devices.reshape(SIZES), AXES)
    dp, mp = AXES[:2], AXES[2:]
    in_specs = (P(dp, mp), P(dp, mp), P(mp, dp, None))
    out_specs = (P(mp, None, dp), P(mp, dp, None))
    return jax.shard_map(
        per_device, mesh=fine, in_specs=in_specs, out_specs=out_specs, check_vma=False
    )
```

```python
import jax
import jax.numpy as jnp
from jax import lax
from jax.experimental import pallas as pl
from jax.experimental.pallas import tpu as pltpu
from jax.sharding import Mesh, PartitionSpec as P

NS_ITERS = 8
BLOCK = 1024
RANK = 256
SIZES = (8, 8, 4, 2)
AXES = ("z", "y", "x", "core")
WIDTH = 16
PARTS = 2
BAND = BLOCK // PARTS

NN = (((1,), (0,)), ((), ()))
NT = (((1,), (1,)), ((), ()))

THREE = ((0, 1), (1, 0), (0, 0))
SIX = ((1, 1), (2, 0), (0, 2), (0, 1), (1, 0), (0, 0))


def split(value, count):
    pieces = []
    for step in range(count):
        piece = value.astype(jnp.bfloat16)
        pieces.append(piece)
        if step < count - 1:
            value = value - piece.astype(jnp.float32)
    return pieces


def product(left, right, terms, dims=NN):
    total = None
    for i, j in terms:
        term = lax.dot_general(left[i], right[j], dims, preferred_element_type=jnp.float32)
        total = term if total is None else total + term
    return total


def identity():
    rows = lax.broadcasted_iota(jnp.int32, (RANK, RANK), 0)
    cols = lax.broadcasted_iota(jnp.int32, (RANK, RANK), 1)
    return jnp.where(rows == cols, 1.0, 0.0).astype(jnp.float32)


def trace(matrix, ident):
    return jnp.sum(matrix * ident, keepdims=True)


def own_product(value):
    one, two, three = split(value, 3)
    cross = lax.dot_general(
        jnp.concatenate([one, one], axis=1),
        jnp.concatenate([three, two], axis=1),
        NT,
        preferred_element_type=jnp.float32,
    )
    return (cross + cross.T) + product((one, two), (one, two), ((1, 1), (0, 0)), NT)


def by_halves(left, right):
    half = RANK // 2
    return jnp.concatenate(
        [product([piece[i:i + half] for piece in left], right, THREE) for i in (0, half)]
    )


def inverse_root(matrix, ident, beside=lambda step: None):
    scale = trace(matrix, ident)
    tmat = matrix * (1.0 / scale)
    zmat = ident
    for step in range(NS_ITERS):
        tsp = split(tmat, 2)
        last = step == NS_ITERS - 1
        if not last:
            square = by_halves(tsp, tsp)
        if step == 0:
            zmat = 1.5 * ident - 0.5 * tmat
        else:
            zmat = 1.5 * zmat - 0.5 * by_halves(split(zmat, 2), tsp)
        if not last:
            cube = by_halves(split(square, 2), tsp)
            beside(step + 1)
            tmat = 2.25 * tmat - 1.5 * square + 0.25 * cube
    return zmat * lax.rsqrt(scale)


def full_product(left, right):
    return product(split(left, 3), split(right, 3), SIX)


def few_rows(left, right):
    one, two, three = split(left, 3)
    rows = left.shape[0]
    first = lax.dot_general(
        jnp.concatenate([three, two, one]), right[0], NN, preferred_element_type=jnp.float32
    )
    second = lax.dot_general(
        jnp.concatenate([two, one]), right[1], NN, preferred_element_type=jnp.float32
    )
    third = lax.dot_general(one, right[2], NN, preferred_element_type=jnp.float32)
    low = second[:rows] + third + first[:rows]
    return low + (second[rows:] + first[rows:2 * rows]) + first[2 * rows:]


def finish_kernel(
    place_ref, both_ref, upd_ref, fresh_ref,
    wide_ref, high_ref, low_ref, all_ref, pow_ref, pick_ref, rows_ref, sems,
):
    copies = []
    for part in range(PARTS):
        band = pl.ds(part * BAND, BAND)
        copies.append(pltpu.make_async_copy(both_ref.at[band, :], wide_ref.at[band, :], sems.at[part]))
        copies[-1].start()
    wt = None
    for part in range(PARTS):
        copies[part].wait()
        band = pl.ds(part * BAND, BAND)
        high, low = split(wide_ref[band, :], 2)
        high_ref[band, :] = high
        low_ref[band, :] = low
        skt = wide_ref[band, BLOCK:].T
        term = product(split(skt, 2), (high, low), THREE)
        wt = term if wt is None else wt + term
    block = pl.ds(pl.multiple_of(place_ref[0] * 128, 128), 128)
    inner = pl.ds(pl.multiple_of(place_ref[1] * WIDTH, WIDTH), WIDTH)
    moved = pl.ds(pl.multiple_of(place_ref[2] * 128, 128), 128)

    both = (high_ref[...], low_ref[...])
    lane = lax.broadcasted_iota(jnp.int32, (1, BLOCK + RANK), 1)
    weight = jnp.where(lane < BLOCK, 1.0, 0.95)
    power = product(split(wt * weight, 2), both, THREE, NT)
    ident = identity()
    psp = split(power, 3)
    gram = own_product(power)
    ritz = []

    def beside(step):
        if step <= (BLOCK + RANK) // 256:
            part = pl.ds((step - 1) * 256, 256)
            gpow = product(psp[:2], (high_ref[:, part], low_ref[:, part]), THREE)
            all_ref[:, part] = gpow
            ritz.append(gpow if step <= BLOCK // 256 else gpow * 0.95 ** 0.5)

    cinv = inverse_root(gram, ident, beside)
    ritz = own_product(jnp.concatenate(ritz, axis=1))
    csp = split(cinv, 3)
    pick_ref[...] = wide_ref[:, block].T
    cols = pick_ref[inner, :]
    pow_ref[...] = power
    rows_ref[...] = pow_ref[:, moved].T
    prow = rows_ref[inner, :]
    rows_ref[...] = all_ref[:, block].T
    gcol = rows_ref[inner, :]
    hmat = product(split(product(csp, split(ritz, 3), SIX), 3), csp, SIX)
    eps = trace(hmat, ident) * (0.1 / RANK)
    hdamp = hmat + eps * ident
    held = []

    def late(step):
        if step == 1:
            held.append(few_rows(jnp.concatenate([prow, gcol], axis=0), csp))
        if step == 2:
            held.append(few_rows(held[0][:WIDTH], split(hdamp, 3)))

    rinv = inverse_root(hdamp, ident, late)
    pair, lead = held
    last = few_rows(jnp.concatenate([lead, pair[WIDTH:]], axis=0), split(rinv, 3))
    fresh_ref[...] = last[:WIDTH]
    middle = jnp.sqrt(eps) * last[WIDTH:] - pair[WIDTH:]
    coef = few_rows(middle, csp)
    update = cols + few_rows(coef, psp)
    for natural in range(8):
        ahead, across = natural // 2, natural % 2
        blocks = [update[:, (4 * side + ahead) * 128:(4 * side + ahead + 1) * 128] for side in (0, 1)]
        upd_ref[:, natural * 128:(natural + 1) * 128] = jnp.where(
            place_ref[3] == 0, blocks[across], blocks[1 - across]
        )


def finish(places, both):
    whole = pl.BlockSpec(memory_space=pltpu.VMEM)
    return pl.pallas_call(
        finish_kernel,
        out_shape=(
            jax.ShapeDtypeStruct((WIDTH, BLOCK), jnp.float32),
            jax.ShapeDtypeStruct((WIDTH, RANK), jnp.float32),
        ),
        in_specs=[pl.BlockSpec(memory_space=pltpu.SMEM), pl.BlockSpec(memory_space=pltpu.HBM)],
        out_specs=(whole, whole),
        scratch_shapes=[
            pltpu.VMEM((BLOCK, BLOCK + RANK), jnp.float32),
            pltpu.VMEM((BLOCK, BLOCK + RANK), jnp.bfloat16),
            pltpu.VMEM((BLOCK, BLOCK + RANK), jnp.bfloat16),
            pltpu.VMEM((RANK, BLOCK + RANK), jnp.float32),
            pltpu.VMEM((RANK, BLOCK), jnp.float32),
            pltpu.VMEM((128, BLOCK), jnp.float32),
            pltpu.VMEM((128, RANK), jnp.float32),
            pltpu.SemaphoreType.DMA((PARTS,)),
        ],
        compiler_params=pltpu.CompilerParams(vmem_limit_bytes=60 * 1024 * 1024),
    )(places, both)


def groups(first):
    sets = []
    for x in range(SIZES[2]):
        for other in range(8):
            for core in range(2):
                along_y = (core == 0) == first
                sets.append([
                    (((other * 8 + i) if along_y else (i * 8 + other)) * SIZES[2] + x) * 2 + core
                    for i in range(8)
                ])
    return sets


def sketch_moves():
    nz, ny, nx, nc = SIZES
    moves = []
    for z in range(nz):
        for y in range(ny):
            for x in range(nx):
                for core in range(nc):
                    position, inner = (y, z) if core == 0 else (z, y)
                    natural = position % 4 * 2 + (position // 4 + core) % 2
                    source = ((natural * ny + inner) * nx + x) * nc + core
                    moves.append((source, ((z * ny + y) * nx + x) * nc + core))
    return moves


def exchange(parts, axes, sets=None):
    return lax.all_to_all(
        parts, axes, split_axis=0, concat_axis=0, tiled=True, axis_index_groups=sets
    )


def gather(block, axes, size, sets=None):
    return exchange(jnp.broadcast_to(block[None], (size,) + block.shape), axes, sets)


def per_device(inputs, out_grads, sketch):
    near = gather(inputs, "x", SIZES[2])
    far = lax.ppermute(near, "core", [(0, 1), (1, 0)])
    core = lax.axis_index("core")
    part = lax.dot_general(
        jnp.concatenate([near, far]),
        out_grads,
        (((1,), (0,)), ((), ())),
        preferred_element_type=jnp.float32,
    ).reshape(BLOCK, BLOCK)
    part, own_sk = lax.optimization_barrier((part, sketch[0]))
    one, two = groups(True), groups(False)
    band = lax.psum_scatter(part, AXES, scatter_dimension=0, tiled=True, axis_index_groups=one)
    own_sk = lax.ppermute(own_sk, AXES, sketch_moves())
    own_sk, band = lax.optimization_barrier((own_sk, band))
    rows = jnp.sum(exchange(band.reshape(8, WIDTH, BLOCK), AXES, two), axis=0)
    rows = jnp.concatenate([rows, own_sk], axis=1)
    slab = gather(rows, AXES, 8, two).reshape(8 * WIDTH, BLOCK + RANK)
    both = lax.all_gather(slab, AXES, axis=0, tiled=True, axis_index_groups=one)
    z, y = lax.axis_index("z"), lax.axis_index("y")
    places = jnp.stack([z, y, (z % 2 + core) % 2 * 4 + z // 2, core])
    update, fresh = finish(places.astype(jnp.int32), both)
    return (update.T[None], fresh[None])


def solution(mesh):
    fine = Mesh(mesh.devices.reshape(SIZES), AXES)
    dp, mp = AXES[:2], AXES[2:]
    in_specs = (P(dp, mp), P(dp, mp), P(mp, dp, None))
    out_specs = (P(mp, None, dp), P(mp, dp, None))
    return jax.shard_map(
        per_device, mesh=fine, in_specs=in_specs, out_specs=out_specs, check_vma=False
    )
```

```python
import jax
import jax.numpy as jnp
from jax import lax
from jax.experimental import pallas as pl
from jax.experimental.pallas import tpu as pltpu
from jax.sharding import Mesh, PartitionSpec as P

NS_ITERS = 8
BLOCK = 1024
RANK = 256
SIZES = (8, 8, 4, 2)
AXES = ("z", "y", "x", "core")
WIDTH = 16
PARTS = 2
BAND = BLOCK // PARTS

NN = (((1,), (0,)), ((), ()))
NT = (((1,), (1,)), ((), ()))

THREE = ((0, 1), (1, 0), (0, 0))
SIX = ((1, 1), (2, 0), (0, 2), (0, 1), (1, 0), (0, 0))


def split(value, count):
    pieces = []
    for step in range(count):
        piece = value.astype(jnp.bfloat16)
        pieces.append(piece)
        if step < count - 1:
            value = value - piece.astype(jnp.float32)
    return pieces


def product(left, right, terms, dims=NN):
    total = None
    for i, j in terms:
        term = lax.dot_general(left[i], right[j], dims, preferred_element_type=jnp.float32)
        total = term if total is None else total + term
    return total


def identity():
    rows = lax.broadcasted_iota(jnp.int32, (RANK, RANK), 0)
    cols = lax.broadcasted_iota(jnp.int32, (RANK, RANK), 1)
    return jnp.where(rows == cols, 1.0, 0.0).astype(jnp.float32)


def trace(matrix, ident):
    return jnp.sum(matrix * ident, keepdims=True)


def own_product(value):
    one, two, three = split(value, 3)
    cross = lax.dot_general(
        jnp.concatenate([one, one], axis=1),
        jnp.concatenate([three, two], axis=1),
        NT,
        preferred_element_type=jnp.float32,
    )
    return (cross + cross.T) + product((one, two), (one, two), ((1, 1), (0, 0)), NT)


def by_halves(left, right):
    half = RANK // 2
    return jnp.concatenate(
        [product([piece[i:i + half] for piece in left], right, THREE) for i in (0, half)]
    )


def inverse_root(matrix, ident, beside=lambda step: None):
    scale = trace(matrix, ident)
    tmat = matrix * (1.0 / scale)
    zmat = ident
    for step in range(NS_ITERS):
        tsp = split(tmat, 2)
        last = step == NS_ITERS - 1
        if not last:
            square = by_halves(tsp, tsp)
        if step == 0:
            zmat = 1.5 * ident - 0.5 * tmat
        else:
            zmat = 1.5 * zmat - 0.5 * by_halves(split(zmat, 2), tsp)
        if not last:
            cube = by_halves(split(square, 2), tsp)
            beside(step + 1)
            tmat = 2.25 * tmat - 1.5 * square + 0.25 * cube
    return zmat * lax.rsqrt(scale)


def full_product(left, right):
    return product(split(left, 3), split(right, 3), SIX)


def few_rows(left, right):
    one, two, three = split(left, 3)
    rows = left.shape[0]
    first = lax.dot_general(
        jnp.concatenate([three, two, one]), right[0], NN, preferred_element_type=jnp.float32
    )
    second = lax.dot_general(
        jnp.concatenate([two, one]), right[1], NN, preferred_element_type=jnp.float32
    )
    third = lax.dot_general(one, right[2], NN, preferred_element_type=jnp.float32)
    low = second[:rows] + third + first[:rows]
    return low + (second[rows:] + first[rows:2 * rows]) + first[2 * rows:]


def finish_kernel(
    place_ref, both_ref, upd_ref, fresh_ref,
    wide_ref, high_ref, low_ref, all_ref, pow_ref, pick_ref, rows_ref, sems,
):
    copies = []
    for part in range(PARTS):
        band = pl.ds(part * BAND, BAND)
        copies.append(pltpu.make_async_copy(both_ref.at[band, :], wide_ref.at[band, :], sems.at[part]))
        copies[-1].start()
    wt = None
    for part in range(PARTS):
        copies[part].wait()
        band = pl.ds(part * BAND, BAND)
        high, low = split(wide_ref[band, :], 2)
        high_ref[band, :] = high
        low_ref[band, :] = low
        skt = wide_ref[band, BLOCK:].T
        term = product(split(skt, 2), (high, low), THREE)
        wt = term if wt is None else wt + term
    block = pl.ds(pl.multiple_of(place_ref[0] * 128, 128), 128)
    inner = pl.ds(pl.multiple_of(place_ref[1] * WIDTH, WIDTH), WIDTH)
    moved = pl.ds(pl.multiple_of(place_ref[2] * 128, 128), 128)

    both = (high_ref[...], low_ref[...])
    lane = lax.broadcasted_iota(jnp.int32, (1, BLOCK + RANK), 1)
    weight = jnp.where(lane < BLOCK, 1.0, 0.95)
    power = product(split(wt * weight, 2), both, THREE, NT)
    ident = identity()
    psp = split(power, 3)
    gram = own_product(power)
    ritz = []

    def beside(step):
        if step <= (BLOCK + RANK) // 256:
            part = pl.ds((step - 1) * 256, 256)
            gpow = product(psp[:2], (high_ref[:, part], low_ref[:, part]), THREE)
            all_ref[:, part] = gpow
            ritz.append(gpow if step <= BLOCK // 256 else gpow * 0.95 ** 0.5)

    cinv = inverse_root(gram, ident, beside)
    ritz = own_product(jnp.concatenate(ritz, axis=1))
    csp = split(cinv, 3)
    pick_ref[...] = wide_ref[:, block].T
    cols = pick_ref[inner, :]
    pow_ref[...] = power
    rows_ref[...] = pow_ref[:, moved].T
    prow = rows_ref[inner, :]
    rows_ref[...] = all_ref[:, block].T
    gcol = rows_ref[inner, :]
    hmat = product(split(product(csp, split(ritz, 3), SIX), 3), csp, SIX)
    eps = trace(hmat, ident) * (0.1 / RANK)
    hdamp = hmat + eps * ident
    held = []

    def late(step):
        if step == 1:
            held.append(few_rows(jnp.concatenate([prow, gcol], axis=0), csp))
        if step == 2:
            held.append(few_rows(held[0][:WIDTH], split(hdamp, 3)))

    rinv = inverse_root(hdamp, ident, late)
    pair, lead = held
    last = few_rows(jnp.concatenate([lead, pair[WIDTH:]], axis=0), split(rinv, 3))
    fresh_ref[...] = last[:WIDTH]
    middle = jnp.sqrt(eps) * last[WIDTH:] - pair[WIDTH:]
    coef = few_rows(middle, csp)
    update = cols + few_rows(coef, psp)
    for natural in range(8):
        ahead, across = natural // 2, natural % 2
        blocks = [update[:, (4 * side + ahead) * 128:(4 * side + ahead + 1) * 128] for side in (0, 1)]
        upd_ref[:, natural * 128:(natural + 1) * 128] = jnp.where(
            place_ref[3] == 0, blocks[across], blocks[1 - across]
        )


def finish(places, both):
    whole = pl.BlockSpec(memory_space=pltpu.VMEM)
    return pl.pallas_call(
        finish_kernel,
        out_shape=(
            jax.ShapeDtypeStruct((WIDTH, BLOCK), jnp.float32),
            jax.ShapeDtypeStruct((WIDTH, RANK), jnp.float32),
        ),
        in_specs=[pl.BlockSpec(memory_space=pltpu.SMEM), pl.BlockSpec(memory_space=pltpu.HBM)],
        out_specs=(whole, whole),
        scratch_shapes=[
            pltpu.VMEM((BLOCK, BLOCK + RANK), jnp.float32),
            pltpu.VMEM((BLOCK, BLOCK + RANK), jnp.bfloat16),
            pltpu.VMEM((BLOCK, BLOCK + RANK), jnp.bfloat16),
            pltpu.VMEM((RANK, BLOCK + RANK), jnp.float32),
            pltpu.VMEM((RANK, BLOCK), jnp.float32),
            pltpu.VMEM((128, BLOCK), jnp.float32),
            pltpu.VMEM((128, RANK), jnp.float32),
            pltpu.SemaphoreType.DMA((PARTS,)),
        ],
        compiler_params=pltpu.CompilerParams(vmem_limit_bytes=60 * 1024 * 1024),
    )(places, both)


def groups(first):
    sets = []
    for x in range(SIZES[2]):
        for other in range(8):
            for core in range(2):
                along_y = (core == 0) == first
                sets.append([
                    (((other * 8 + i) if along_y else (i * 8 + other)) * SIZES[2] + x) * 2 + core
                    for i in range(8)
                ])
    return sets


def sketch_moves():
    nz, ny, nx, nc = SIZES
    moves = []
    for z in range(nz):
        for y in range(ny):
            for x in range(nx):
                for core in range(nc):
                    position, inner = (y, z) if core == 0 else (z, y)
                    natural = position % 4 * 2 + (position // 4 + core) % 2
                    source = ((natural * ny + inner) * nx + x) * nc + core
                    moves.append((source, ((z * ny + y) * nx + x) * nc + core))
    return moves


def exchange(parts, axes, sets=None):
    return lax.all_to_all(
        parts, axes, split_axis=0, concat_axis=0, tiled=True, axis_index_groups=sets
    )


def gather(block, axes, size, sets=None):
    return exchange(jnp.broadcast_to(block[None], (size,) + block.shape), axes, sets)


def per_device(inputs, out_grads, sketch):
    near = gather(inputs, "x", SIZES[2])
    far = lax.ppermute(near, "core", [(0, 1), (1, 0)])
    core = lax.axis_index("core")
    part = lax.dot_general(
        jnp.concatenate([near, far]),
        out_grads,
        (((1,), (0,)), ((), ())),
        preferred_element_type=jnp.float32,
    ).reshape(BLOCK, BLOCK)
    part, own_sk = lax.optimization_barrier((part, sketch[0]))
    one, two = groups(True), groups(False)
    band = lax.psum_scatter(part, AXES, scatter_dimension=0, tiled=True, axis_index_groups=one)
    own_sk = lax.ppermute(own_sk, AXES, sketch_moves())
    own_sk = gather(own_sk, AXES, 8, two).reshape(8 * WIDTH, RANK)
    own_sk, band = lax.optimization_barrier((own_sk, band))
    rows = jnp.sum(exchange(band.reshape(8, WIDTH, BLOCK), AXES, two), axis=0)
    slab = gather(rows, AXES, 8, two).reshape(8 * WIDTH, BLOCK)
    slab = jnp.concatenate([slab, own_sk], axis=1)
    both = lax.all_gather(slab, AXES, axis=0, tiled=True, axis_index_groups=one)
    z, y = lax.axis_index("z"), lax.axis_index("y")
    places = jnp.stack([z, y, (z % 2 + core) % 2 * 4 + z // 2, core])
    update, fresh = finish(places.astype(jnp.int32), both)
    return (update.T[None], fresh[None])


def solution(mesh):
    fine = Mesh(mesh.devices.reshape(SIZES), AXES)
    dp, mp = AXES[:2], AXES[2:]
    in_specs = (P(dp, mp), P(dp, mp), P(mp, dp, None))
    out_specs = (P(mp, None, dp), P(mp, dp, None))
    return jax.shard_map(
        per_device, mesh=fine, in_specs=in_specs, out_specs=out_specs, check_vma=False
    )
```
